32 devices in a mesh: dom: 16 (over z, y, x), rhs: 2 (over core).
Axes of the slice: x: 2, y: 2, z: 4, core: 2. Of those that a mesh axis runs over, the one named last changes fastest.
Arguments:
- jacobian: bfloat16 [128, 7, 162, 162], P('dom'), may hold values from -0.1875 to 0.1875
- block_weight: bfloat16 [128, 162, 162], P('dom'), may hold values from -0.5 to 0.5
- rhs_grad: float32 [128, 16, 162], P('dom', 'rhs')
- flow_residual: float32 [128, 162], P('dom'), may hold values from -6 to 6
- face_nbr: int32 [128, 6], P('dom'), may hold values from 0 to 11, as said below
- send_list: int32 [16, 2, 2], P('dom'), may hold values from 0 to 7, as said below
Outputs:
- adjoint: float32 [128, 16, 162], P('dom', 'rhs')
- residual_check: float32 [128, 16, 162], P('dom', 'rhs')
- indicator: float32 [128], P('dom')
The draws below stay inside these ranges and needn't reach their ends.
Inputs may be any that keep to these rules, and one draw needn't show every extreme that they name: `face_nbr`: A value m < 8 names an element of the same partition; 8 + s with s < 2 names slot s of list 1 of the partition below; 10 + s names slot s of list 0 of the partition above. The first partition never uses the range below and the last never the range above. `send_list`: the 4 entries of one partition's two lists are distinct local element indices.
All inputs are finite; a program needn't handle non-finite values.
Results may differ from the reference program's by a relative error of at most 0.008.
Values may be sent and summed in bfloat16 or wider, within the bound.
A program may use at most 64 MiB of HBM per device.

```python
import jax
import jax.numpy as jnp
from jax import lax

NB = 162
NFACE = 6
RHS = 16
ITERS = 2
E_DEV = 8
CAP = 2
PARTS_SIZE = 16
ELEMS = 128
N_DOM = 16


def draw_rhs_grad(key, part):
    position = jnp.arange(ELEMS)
    factor = 1.0 + 2.0 * (position // E_DEV).astype(jnp.float32) / float(N_DOM - 1)
    base = jax.random.normal(key, (ELEMS, RHS, NB), jnp.float32)
    return (base * factor[:, None, None]).astype(jnp.float32)


def draw_face_nbr(key, part):
    values = jax.random.randint(key, (ELEMS, NFACE), 0, E_DEV + 2 * CAP)
    position = jnp.arange(ELEMS)
    device = (position // E_DEV)[:, None]
    local = (position % E_DEV)[:, None]
    faces = jnp.arange(NFACE)[None, :]
    corner = (local == E_DEV - 1) & (faces == NFACE - 1)
    values = jnp.where(corner, E_DEV + 2 * CAP - 1, values)
    first_ghost = (device == 1) & (local == 0) & (faces == 0)
    values = jnp.where(first_ghost, E_DEV, values)
    lower_bad = (device == 0) & (values >= E_DEV) & (values < E_DEV + CAP)
    upper_bad = (device == N_DOM - 1) & (values >= E_DEV + CAP)
    values = jnp.where(lower_bad | upper_bad, local, values)
    return values.astype(jnp.int32)


def draw_send_list(key, part):
    columns = jnp.arange(E_DEV)
    scores = jax.random.randint(key, (PARTS_SIZE, E_DEV), 0, 2 ** 20) * E_DEV + columns[None, :]
    boosted = (jnp.arange(PARTS_SIZE)[:, None] == 0) & ((columns == 0) | (columns == E_DEV - 1))[None, :]
    scores = jnp.where(boosted, 2 ** 20 * E_DEV + (E_DEV - 1 - columns)[None, :], scores)
    order = jnp.argsort(-scores, axis=1, stable=True)
    return order[:, :2 * CAP].reshape(PARTS_SIZE, 2, CAP).astype(jnp.int32)


def level_of(own_key, dims, pieces, smallest, high):
    loudness = 1.0
    for dim, shards_of in pieces:
        steps = jax.random.uniform(jax.random.fold_in(jax.random.fold_in(own_key, 6), dim), (shards_of,), jnp.float32, smallest / len(pieces), high / len(pieces))
        loudness = loudness * jnp.repeat(jnp.exp(steps), dims[dim] // shards_of).reshape((-1,) + (1,) * (len(dims) - 1 - dim))
    return loudness


def bell_draw(key, shape, scale, bound, pieces=(), kind=jnp.bfloat16):
    drawn = scale * jax.random.normal(key, shape, jnp.float32)
    if pieces:
        drawn = drawn * level_of(key, shape, pieces, -0.22, 0.18)
    return jnp.clip(drawn, -bound, bound).astype(kind)


def setup_inputs(seed: int = 0) -> dict:
    key_of = jax.random.split(jax.random.key(seed), 7)
    return {
        "jacobian": bell_draw(key_of[0], (ELEMS, NFACE + 1, NB, NB), (7 * NB) ** -0.5, 0.1875, ((0, 16),)),
        "block_weight": bell_draw(key_of[1], (ELEMS, NB, NB), NB ** -0.5, 0.5, ((0, 16),)),
        "rhs_grad": draw_rhs_grad(jax.random.fold_in(key_of[6], 71), 0),
        "flow_residual": bell_draw(key_of[3], (ELEMS, NB), 1.0, 6.0, ((0, 16),), jnp.float32),
        "face_nbr": draw_face_nbr(jax.random.fold_in(key_of[6], 71), 0),
        "send_list": draw_send_list(jax.random.fold_in(key_of[6], 71), 0),
    }


epsilon = 1e-06

def neighbours(face_nbr, send_list):
    position = jnp.arange(ELEMS, dtype=jnp.int32)
    device = (position // E_DEV)[:, None]
    below = jnp.clip(device - 1, 0, N_DOM - 1).astype(jnp.int32)
    above = jnp.clip(device + 1, 0, N_DOM - 1).astype(jnp.int32)
    low_slot = jnp.clip(face_nbr - E_DEV, 0, CAP - 1).astype(jnp.int32)
    high_slot = jnp.clip(face_nbr - E_DEV - CAP, 0, CAP - 1).astype(jnp.int32)
    local_ids = device * E_DEV + face_nbr
    low_ids = below * E_DEV + send_list[below, 1, low_slot]
    high_ids = above * E_DEV + send_list[above, 0, high_slot]
    chosen = jnp.where(face_nbr < E_DEV, local_ids, jnp.where(face_nbr < E_DEV + CAP, low_ids, high_ids))
    return chosen.astype(jnp.int32)

def forward_block(operands):
    blocks, vectors = operands
    return jnp.einsum('ekij,ekrj->eri', blocks.astype(jnp.float32), vectors.astype(jnp.float32), precision=lax.Precision.HIGHEST)

def backward_block(operands):
    blocks, vectors = operands
    return jnp.einsum('ekij,eri->ekrj', blocks.astype(jnp.float32), vectors.astype(jnp.float32), precision=lax.Precision.HIGHEST)

def operate(field, jacobian, block_weight, nbr):
    rounded = field.astype(jnp.bfloat16)
    beside_all = rounded[nbr]
    stacked = jnp.concatenate([rounded[:, None], beside_all], axis=1)
    jac_parts = jacobian.reshape(N_DOM, E_DEV, NFACE + 1, NB, NB)
    image = lax.map(forward_block, (jac_parts, stacked.reshape(N_DOM, E_DEV, NFACE + 1, RHS, NB)))
    image = image.reshape(ELEMS, RHS, NB).astype(jnp.bfloat16)
    scaled = jnp.einsum('eij,erj->eri', block_weight.astype(jnp.float32), image.astype(jnp.float32), precision=lax.Precision.HIGHEST).astype(jnp.bfloat16)
    terms = lax.map(backward_block, (jac_parts, scaled.reshape(N_DOM, E_DEV, RHS, NB)))
    terms = terms.reshape(ELEMS, NFACE + 1, RHS, NB)
    spread = jax.ops.segment_sum(terms[:, 1:].reshape(ELEMS * NFACE, RHS, NB), nbr.reshape(-1), num_segments=ELEMS)
    return terms[:, 0] + spread

def inner(first, second):
    return lax.optimization_barrier(jnp.sum(first * second, axis=(0, 2)))

def least_squares(beta, hess):
    target = [beta] + [jnp.zeros_like(beta)] * ITERS
    cosines = []
    sines = []
    upper = {}
    for column in range(ITERS):
        entries = [hess[row, column] for row in range(column + 2)]
        for row in range(column):
            first = cosines[row] * entries[row] + sines[row] * entries[row + 1]
            second = -sines[row] * entries[row] + cosines[row] * entries[row + 1]
            entries[row] = first
            entries[row + 1] = second
        radius = jnp.sqrt(entries[column] * entries[column] + entries[column + 1] * entries[column + 1])
        cosine = entries[column] / radius
        sine = entries[column + 1] / radius
        cosines.append(cosine)
        sines.append(sine)
        for row in range(column):
            upper[row, column] = entries[row]
        upper[column, column] = radius
        current = target[column]
        target[column] = cosine * current
        target[column + 1] = -sine * current
    coeffs = [jnp.zeros_like(beta)] * ITERS
    for row in reversed(range(ITERS)):
        partial_sum = target[row]
        for later in range(row + 1, ITERS):
            partial_sum = partial_sum - upper[row, later] * coeffs[later]
        coeffs[row] = partial_sum / upper[row, row]
    return coeffs

def reference(jacobian, block_weight, rhs_grad, flow_residual, face_nbr, send_list):
    nbr = neighbours(face_nbr, send_list)
    beta = jnp.sqrt(inner(rhs_grad, rhs_grad) + epsilon)
    basis = [rhs_grad / beta[None, :, None]]
    raws = []
    hess = {}
    for column in range(ITERS):
        work = operate(basis[column], jacobian, block_weight, nbr)
        raws.append(work)
        for row in range(column + 1):
            factor = inner(basis[row], work)
            hess[row, column] = factor
            work = work - factor[None, :, None] * basis[row]
        length = jnp.sqrt(inner(work, work) + epsilon)
        hess[column + 1, column] = length
        if column + 1 < ITERS:
            basis.append(work / length[None, :, None])
    coeffs = least_squares(beta, hess)
    adjoint = jnp.zeros_like(rhs_grad)
    recurrence = rhs_grad
    for column in range(ITERS):
        adjoint = adjoint + coeffs[column][None, :, None] * basis[column]
        recurrence = recurrence - coeffs[column][None, :, None] * raws[column]
    refined = adjoint + recurrence
    residual_check = rhs_grad - operate(refined, jacobian, block_weight, nbr)
    indicator = lax.optimization_barrier(jnp.sum(jnp.abs(lax.optimization_barrier(jnp.sum(adjoint * flow_residual[:, None, :], axis=2))), axis=1))
    return (adjoint, residual_check, indicator)
```

```python
import functools

import jax
import jax.numpy as jnp
from jax import lax
from jax.experimental import pallas as pl
from jax.experimental.pallas import tpu as pltpu
from jax.sharding import PartitionSpec as P

EPSILON = 1e-06
MESH = pl.DeviceIdType.MESH
F32 = jnp.float32
BF16 = jnp.bfloat16


def radices_of(n):
    out = []
    while n > 1:
        for r in (4, 2, 3, 5, 7):
            if n % r == 0:
                out.append(r)
                n //= r
                break
        else:
            out.append(n)
            n = 1
    return out


def dot_rows(rows, block):
    return lax.dot_general(rows, block, (((1,), (0,)), ((), ())), preferred_element_type=F32)


def dot_rows_t(rows, block):
    return lax.dot_general(rows, block, (((1,), (1,)), ((), ())), preferred_element_type=F32)


def coefficients(beta, b, c, d, e, f, g):
    h11 = c
    w_sq = d - 2.0 * h11 * c + h11 * h11 * b
    h21 = jnp.sqrt(jnp.maximum(w_sq, 0.0) + EPSILON)
    s = 1.0 / h21
    h12 = s * (e - h11 * c)
    v2v1 = s * (c - h11 * b)
    v2v2 = s * s * w_sq
    v2raw2 = s * s * (f - h11 * d - h11 * e + h11 * h11 * c)
    raw2sq = s * s * (g - 2.0 * h11 * f + h11 * h11 * d)
    h22 = v2raw2 - h12 * v2v1
    last = (
        raw2sq
        + h12 * h12 * b
        + h22 * h22 * v2v2
        - 2.0 * h12 * h12
        - 2.0 * h22 * v2raw2
        + 2.0 * h12 * h22 * v2v1
    )
    h32 = jnp.sqrt(jnp.maximum(last, 0.0) + EPSILON)
    radius = jnp.sqrt(h11 * h11 + h21 * h21)
    cos1, sin1 = h11 / radius, h21 / radius
    t1, t2 = cos1 * beta, -sin1 * beta
    upper = cos1 * h12 + sin1 * h22
    low = -sin1 * h12 + cos1 * h22
    radius2 = jnp.sqrt(low * low + h32 * h32)
    t2 = (low / radius2) * t2
    c2 = t2 / radius2
    c1 = (t1 - upper * c2) / radius
    return c1 - c2 * s * h11, c2 * s


def kernel(
    n, radices,
    jac_hbm, wgt_hbm, rhs_ref, flow_ref, nbr_ref, list_ref,
    adj_ref, res_ref, ind_ref,
    jac, wgt, xs, up, hsend, hrecv, asend, arecv, isend, irecv,
    jsem, wsem, hs_sem, hr_sem, as_sem, ar_sem, is_sem, ir_sem,
):
    elements, faces1 = jac.shape[0], jac.shape[1]
    cap = list_ref.shape[2]
    slots = elements + 2 * cap
    me = lax.axis_index("dom")
    core = lax.axis_index("rhs")
    cores = lax.axis_size("rhs")

    jcopies = [pltpu.make_async_copy(jac_hbm.at[e], jac.at[e], jsem.at[e]) for e in range(elements)]
    wcopy = pltpu.make_async_copy(wgt_hbm, wgt, wsem)
    for copy in jcopies:
        copy.start()
    wcopy.start()

    strides = []
    stride = 1
    for radix in radices:
        strides.append(stride)
        stride *= radix

    def partner(stage, offset):
        radix, step = radices[stage], strides[stage]
        digit = lax.rem(lax.div(me, step), radix)
        return me + (lax.rem(digit + offset, radix) - digit) * step

    barrier = pltpu.get_barrier_semaphore()
    total = cores - 1
    for stage, radix in enumerate(radices):
        for offset in range(1, radix):
            pl.semaphore_signal(barrier, inc=1, device_id=(partner(stage, offset), core), device_id_type=MESH)
            total += 1
    for o in range(1, cores):
        pl.semaphore_signal(barrier, inc=1, device_id=(me, lax.rem(core + o, cores)), device_id_type=MESH)

    @pl.when(me > 0)
    def _():
        pl.semaphore_signal(barrier, inc=1, device_id=(me - 1, core), device_id_type=MESH)

    @pl.when(me < n - 1)
    def _():
        pl.semaphore_signal(barrier, inc=1, device_id=(me + 1, core), device_id_type=MESH)

    rows_shape = rhs_ref.shape[1:]

    @pl.when(me == 0)
    def _():
        hrecv[:, 0] = jnp.zeros((4, 2 * cap) + rows_shape, F32)

    @pl.when(me == n - 1)
    def _():
        hrecv[:, 1] = jnp.zeros((4, 2 * cap) + rows_shape, F32)

    lists = [[list_ref[0, side, s] for s in range(cap)] for side in range(2)]
    nbr = [[nbr_ref[e, k] for k in range(faces1 - 1)] for e in range(elements)]

    ranges = ((0, cap), (0, 2 * cap), (0, 2 * cap), (cap, cap))

    def halo(t, side):
        first, count = ranges[t]
        target = me - 1 if side == 0 else me + 1
        return pltpu.make_async_remote_copy(
            src_ref=hsend.at[t, side, pl.ds(first, count)],
            dst_ref=hrecv.at[t, 1 - side, pl.ds(first, count)],
            send_sem=hs_sem.at[t, side],
            recv_sem=hr_sem.at[t, 1 - side],
            device_id=(target, core),
            device_id_type=MESH,
        )

    def halo_start(t):
        @pl.when(me > 0)
        def _():
            halo(t, 0).start()

        @pl.when(me < n - 1)
        def _():
            halo(t, 1).start()

    def halo_wait(t):
        @pl.when(me > 0)
        def _():
            halo(t, 1).wait_recv()

        @pl.when(me < n - 1)
        def _():
            halo(t, 0).wait_recv()

    def halo_finish(t):
        @pl.when(me > 0)
        def _():
            halo(t, 0).wait_send()

        @pl.when(me < n - 1)
        def _():
            halo(t, 1).wait_send()

    def reduce_copies(q, stage):
        return [
            pltpu.make_async_remote_copy(
                src_ref=asend.at[q, stage],
                dst_ref=arecv.at[q, stage, o - 1],
                send_sem=as_sem.at[q, stage, o - 1],
                recv_sem=ar_sem.at[q, stage, o - 1],
                device_id=(partner(stage, o), core),
                device_id_type=MESH,
            )
            for o in range(1, radices[stage])
        ]

    def reduce_start(q, stage, value):
        asend[q, stage] = value
        for copy in reduce_copies(q, stage):
            copy.start()

    def reduce_end(q, stage):
        for copy in reduce_copies(q, stage):
            copy.wait()
        value = asend[q, stage]
        for o in range(1, radices[stage]):
            value = value + arecv[q, stage, o - 1]
        return value

    stages = len(radices)
    lane = lax.broadcasted_iota(jnp.int32, asend.shape[2:], 1)

    def packed(columns):
        out = jnp.zeros(asend.shape[2:], F32)
        for i, column in enumerate(columns):
            out = jnp.where(lane == i, column, out)
        return out

    def inner(pairs):
        acc = None
        for a, b in pairs:
            acc = a * b if acc is None else acc + a * b
        return jnp.sum(acc, axis=1, keepdims=True)

    r = [rhs_ref[e] for e in range(elements)]
    b_part = packed([inner([(v, v) for v in r])])
    for side in range(2):
        for s in range(cap):
            hsend[0, side, s] = rhs_ref[lists[side][s]]
    for e in range(elements):
        xs[0, e] = r[e]

    pl.semaphore_wait(barrier, total + jnp.where(me > 0, 1, 0) + jnp.where(me < n - 1, 1, 0))
    halo_start(0)
    reduce_start(0, 0, b_part)

    def forward(t, wait_blocks=False):
        y = []
        for e in range(elements):
            if wait_blocks:
                jcopies[e].wait()
            acc = dot_rows_t(xs[t, e].astype(BF16), jac[e, 0])
            for k in range(1, faces1):
                acc = acc + dot_rows_t(xs[t, nbr[e][k - 1]].astype(BF16), jac[e, k])
            y.append(acc.astype(BF16))
        if wait_blocks:
            wcopy.wait()
        return [dot_rows_t(y[e], wgt[e]).astype(BF16) for e in range(elements)]

    def backward(z):
        acc = [jnp.zeros(rows_shape, F32) for _ in range(slots)]
        for e in range(elements):
            acc[e] = acc[e] + dot_rows(z[e], jac[e, 0])
            for k in range(1, faces1):
                term = dot_rows(z[e], jac[e, k])
                for m in range(slots):
                    acc[m] = acc[m] + jnp.where(nbr[e][k - 1] == m, term, 0.0)
        return acc

    def send_partials(t, acc):
        for m in range(slots):
            up[t, m] = acc[m]
        for side in range(2):
            for s in range(cap):
                if t < 3:
                    hsend[t, side, s] = up[t, lists[side][s]]
                hsend[t, side, cap + s] = acc[elements + side * cap + s]
        halo_start(t)

    def merged(t, m):
        value = up[t, m]
        for side in range(2):
            for s in range(cap):
                value = value + jnp.where(lists[side][s] == m, hrecv[t, side, cap + s], 0.0)
        return value

    def receive_partials(t):
        for m in range(elements):
            xs[t, m] = merged(t, m)
        for side in range(2):
            for s in range(cap):
                m = elements + side * cap + s
                xs[t, m] = up[t, m] + hrecv[t, side, s]

    halo_wait(0)
    for side in range(2):
        for s in range(cap):
            xs[0, elements + side * cap + s] = hrecv[0, side, s]
    z = forward(0, True)
    for stage in range(stages - 1):
        reduce_start(0, stage + 1, reduce_end(0, stage))
    acc = backward(z)
    b_sum = reduce_end(0, stages - 1)[:, 0:1]
    beta = jnp.sqrt(b_sum + EPSILON)
    scale = 1.0 / beta
    send_partials(1, [a * scale for a in acc])
    halo_wait(1)
    receive_partials(1)
    acc = backward(forward(1))
    send_partials(2, acc)
    halo_wait(2)
    receive_partials(2)
    span = range(elements)
    v1 = [rhs_ref[e] * scale for e in span]
    raw = [xs[1, e] for e in span]
    u2 = [xs[2, e] for e in span]
    grams = packed(
        [
            inner(zip(v1, raw)),
            inner(zip(raw, raw)),
            inner(zip(v1, u2)),
            inner(zip(raw, u2)),
            inner(zip(u2, u2)),
        ]
    )
    reduce_start(1, 0, grams)
    z = forward(2)
    for stage in range(stages - 1):
        reduce_start(1, stage + 1, reduce_end(1, stage))
    acc = backward(z)
    send_partials(3, acc)
    sums = reduce_end(1, stages - 1)
    c, d, e_, f, g = [sums[:, i : i + 1] for i in range(5)]
    a0, a1 = coefficients(beta, b_sum * scale * scale, c, d, e_, f, g)
    a0s = a0 * scale
    ind = jnp.zeros(isend.shape[1:], F32)
    ilane = lax.broadcasted_iota(jnp.int32, isend.shape[1:], 1)
    for e in span:
        adjoint = a0s * rhs_ref[e] + a1 * xs[1, e]
        adj_ref[e] = adjoint
        term = jnp.abs(jnp.sum(adjoint * flow_ref[pl.ds(e, 1), :], axis=1, keepdims=True))
        ind = jnp.where(ilane == e, jnp.sum(term, axis=0, keepdims=True), ind)
    isend[0] = ind
    icopies = [
        pltpu.make_async_remote_copy(
            src_ref=isend.at[0],
            dst_ref=irecv.at[o - 1],
            send_sem=is_sem.at[o - 1],
            recv_sem=ir_sem.at[o - 1],
            device_id=(me, lax.rem(core + o, cores)),
            device_id_type=MESH,
        )
        for o in range(1, cores)
    ]
    for copy in icopies:
        copy.start()
    k1 = beta + a0
    k2 = a1 - a0
    halo_wait(3)
    for e in span:
        res_ref[e] = rhs_ref[e] - (k1 * xs[1, e] + k2 * xs[2, e] - a1 * merged(3, e))
    for copy in icopies:
        copy.wait()
    for o in range(1, cores):
        ind = ind + irecv[o - 1]
    ind_ref[...] = ind[0:1, 0:elements]
    for t in range(4):
        halo_finish(t)


def per_device(n, jacobian, block_weight, rhs_grad, flow_residual, face_nbr, send_list):
    elements = jacobian.shape[0]
    rows = rhs_grad.shape[1:]
    cap = send_list.shape[2]
    slots = elements + 2 * cap
    radices = radices_of(n)
    stages, widest = len(radices), max(radices)
    cores = lax.axis_size("rhs")
    vmem = pl.BlockSpec(memory_space=pltpu.VMEM)
    smem = pl.BlockSpec(memory_space=pltpu.SMEM)
    anywhere = pl.BlockSpec(memory_space=pl.ANY)
    adjoint, residual, indicator = pl.pallas_call(
        functools.partial(kernel, n, radices),
        out_shape=(
            jax.ShapeDtypeStruct(rhs_grad.shape, F32),
            jax.ShapeDtypeStruct(rhs_grad.shape, F32),
            jax.ShapeDtypeStruct((1, elements), F32),
        ),
        in_specs=[anywhere, anywhere, vmem, vmem, smem, smem],
        out_specs=(vmem, vmem, vmem),
        scratch_shapes=[
            pltpu.VMEM(jacobian.shape, BF16),
            pltpu.VMEM(block_weight.shape, BF16),
            pltpu.VMEM((3, slots) + rows, F32),
            pltpu.VMEM((4, slots) + rows, F32),
            pltpu.VMEM((4, 2, 2 * cap) + rows, F32),
            pltpu.VMEM((4, 2, 2 * cap) + rows, F32),
            pltpu.VMEM((2, stages, rows[0], 128), F32),
            pltpu.VMEM((2, stages, widest - 1, rows[0], 128), F32),
            pltpu.VMEM((1, 8, 128), F32),
            pltpu.VMEM((max(cores - 1, 1), 8, 128), F32),
            pltpu.SemaphoreType.DMA((elements,)),
            pltpu.SemaphoreType.DMA,
            pltpu.SemaphoreType.DMA((4, 2)),
            pltpu.SemaphoreType.DMA((4, 2)),
            pltpu.SemaphoreType.DMA((2, stages, widest - 1)),
            pltpu.SemaphoreType.DMA((2, stages, widest - 1)),
            pltpu.SemaphoreType.DMA((max(cores - 1, 1),)),
            pltpu.SemaphoreType.DMA((max(cores - 1, 1),)),
        ],
        compiler_params=pltpu.CompilerParams(
            collective_id=0, has_side_effects=True, vmem_limit_bytes=40 * 2**20
        ),
    )(jacobian, block_weight, rhs_grad, flow_residual, face_nbr, send_list)
    return adjoint, residual, indicator.reshape(elements)


def solution(mesh):
    in_specs = (
        P("dom", None, None, None),
        P("dom", None, None),
        P("dom", "rhs", None),
        P("dom", None),
        P("dom", None),
        P("dom", None, None),
    )
    out_specs = (P("dom", "rhs", None), P("dom", "rhs", None), P("dom"))
    return jax.shard_map(
        functools.partial(per_device, mesh.shape["dom"]),
        mesh=mesh,
        in_specs=in_specs,
        out_specs=out_specs,
        check_vma=False,
    )
```

```python
import functools

import jax
import jax.numpy as jnp
from jax import lax
from jax.experimental import pallas as pl
from jax.experimental.pallas import tpu as pltpu
from jax.sharding import PartitionSpec as P

EPSILON = 1e-06
MESH = pl.DeviceIdType.MESH
F32 = jnp.float32
BF16 = jnp.bfloat16


def radices_of(n):
    out = []
    while n > 1:
        for r in (4, 2, 3, 5, 7):
            if n % r == 0:
                out.append(r)
                n //= r
                break
        else:
            out.append(n)
            n = 1
    return out


def dot_rows(rows, block):
    return lax.dot_general(rows, block, (((1,), (0,)), ((), ())), preferred_element_type=F32)


def coefficients(beta, b, c, d, e, f, g):
    h11 = c
    w_sq = d - 2.0 * h11 * c + h11 * h11 * b
    h21 = jnp.sqrt(jnp.maximum(w_sq, 0.0) + EPSILON)
    s = 1.0 / h21
    h12 = s * (e - h11 * c)
    v2v1 = s * (c - h11 * b)
    v2v2 = s * s * w_sq
    v2raw2 = s * s * (f - h11 * d - h11 * e + h11 * h11 * c)
    raw2sq = s * s * (g - 2.0 * h11 * f + h11 * h11 * d)
    h22 = v2raw2 - h12 * v2v1
    last = (
        raw2sq
        + h12 * h12 * b
        + h22 * h22 * v2v2
        - 2.0 * h12 * h12
        - 2.0 * h22 * v2raw2
        + 2.0 * h12 * h22 * v2v1
    )
    h32 = jnp.sqrt(jnp.maximum(last, 0.0) + EPSILON)
    radius = jnp.sqrt(h11 * h11 + h21 * h21)
    cos1, sin1 = h11 / radius, h21 / radius
    t1, t2 = cos1 * beta, -sin1 * beta
    upper = cos1 * h12 + sin1 * h22
    low = -sin1 * h12 + cos1 * h22
    radius2 = jnp.sqrt(low * low + h32 * h32)
    t2 = (low / radius2) * t2
    c2 = t2 / radius2
    c1 = (t1 - upper * c2) / radius
    return c1 - c2 * s * h11, c2 * s


def kernel(
    n, radices,
    jac_hbm, wgt_hbm, rhs_ref, flow_ref, nbr_ref, list_ref,
    adj_ref, res_ref, ind_ref,
    jraw, wraw, jac, jac_t, wgt_t, left, right, xs, up, hsend, hrecv, asend, arecv, isend, irecv,
    jsem, wsem, hs_sem, hr_sem, as_sem, ar_sem, is_sem, ir_sem,
):
    faces1, elements = jac.shape[0], jac.shape[1]
    width = jac.shape[2]
    half = left.shape[1]
    cap = list_ref.shape[2]
    slots = elements + 2 * cap
    me = lax.axis_index("dom")
    core = lax.axis_index("rhs")
    cores = lax.axis_size("rhs")

    for k in range(faces1):
        pltpu.make_async_copy(jac_hbm.at[k], jraw.at[k], jsem.at[k]).start()
    wcopy = pltpu.make_async_copy(wgt_hbm, wraw, wsem)
    wcopy.start()

    strides = []
    stride = 1
    for radix in radices:
        strides.append(stride)
        stride *= radix

    def partner(stage, offset):
        radix, step = radices[stage], strides[stage]
        digit = lax.rem(lax.div(me, step), radix)
        return me + (lax.rem(digit + offset, radix) - digit) * step

    stages = len(radices)

    def peers(stage):
        spread = cores if stage == stages - 1 else 1
        out = []
        for offset in range(radices[stage]):
            for other in range(spread):
                if offset or other:
                    target = partner(stage, offset) if offset else me
                    out.append((offset, other, (target, lax.rem(core + other, cores))))
        return out

    barrier = pltpu.get_barrier_semaphore()
    total = 0
    for stage in range(stages):
        for _, _, target in peers(stage):
            pl.semaphore_signal(barrier, inc=1, device_id=target, device_id_type=MESH)
            total += 1

    @pl.when(me > 0)
    def _():
        pl.semaphore_signal(barrier, inc=1, device_id=(me - 1, core), device_id_type=MESH)

    @pl.when(me < n - 1)
    def _():
        pl.semaphore_signal(barrier, inc=1, device_id=(me + 1, core), device_id_type=MESH)

    rows_shape = rhs_ref.shape[1:]

    @pl.when(me == 0)
    def _():
        hrecv[:, 0] = jnp.zeros((4, 2 * cap) + rows_shape, F32)

    @pl.when(me == n - 1)
    def _():
        hrecv[:, 1] = jnp.zeros((4, 2 * cap) + rows_shape, F32)

    lists = [[list_ref[0, side, s] for s in range(cap)] for side in range(2)]
    nbr = [[nbr_ref[e, k] for k in range(faces1 - 1)] for e in range(elements)]

    ranges = ((0, cap), (0, 2 * cap), (0, 2 * cap), (cap, cap))

    def halo(t, side):
        first, count = ranges[t]
        target = me - 1 if side == 0 else me + 1
        return pltpu.make_async_remote_copy(
            src_ref=hsend.at[t, side, pl.ds(first, count)],
            dst_ref=hrecv.at[t, 1 - side, pl.ds(first, count)],
            send_sem=hs_sem.at[t, side],
            recv_sem=hr_sem.at[t, 1 - side],
            device_id=(target, core),
            device_id_type=MESH,
        )

    def halo_start(t):
        @pl.when(me > 0)
        def _():
            halo(t, 0).start()

        @pl.when(me < n - 1)
        def _():
            halo(t, 1).start()

    def halo_wait(t):
        @pl.when(me > 0)
        def _():
            halo(t, 1).wait_recv()

        @pl.when(me < n - 1)
        def _():
            halo(t, 0).wait_recv()

    def halo_finish(t):
        @pl.when(me > 0)
        def _():
            halo(t, 0).wait_send()

        @pl.when(me < n - 1)
        def _():
            halo(t, 1).wait_send()

    def reduce_copies(q, stage):
        return [
            pltpu.make_async_remote_copy(
                src_ref=asend.at[q, stage],
                dst_ref=arecv.at[q, stage, other, offset],
                send_sem=as_sem.at[q, stage, other, offset],
                recv_sem=ar_sem.at[q, stage, other, offset],
                device_id=target,
                device_id_type=MESH,
            )
            for offset, other, target in peers(stage)
        ]

    def reduce_start(q, stage, value):
        asend[q, stage] = value
        for copy in reduce_copies(q, stage):
            copy.start()

    def reduce_end(q, stage):
        for copy in reduce_copies(q, stage):
            copy.wait()
        sums = []
        for other in range(cores if stage == stages - 1 else 1):
            value = arecv[q, stage, other, 0] if other else asend[q, stage]
            for offset in range(1, radices[stage]):
                value = value + arecv[q, stage, other, offset]
            sums.append(value)
        return sums

    lane = lax.broadcasted_iota(jnp.int32, asend.shape[2:], 1)

    def packed(columns):
        out = jnp.zeros(asend.shape[2:], F32)
        for i, column in enumerate(columns):
            out = jnp.where(lane == i, column, out)
        return out

    def inner(pairs):
        acc = None
        for a, b in pairs:
            acc = a * b if acc is None else acc + a * b
        return jnp.sum(acc, axis=1, keepdims=True)

    r = [rhs_ref[e] for e in range(elements)]
    b_part = packed([inner([(v, v) for v in r])])
    for side in range(2):
        for s in range(cap):
            hsend[0, side, s] = rhs_ref[lists[side][s]]
    for e in range(elements):
        xs[0, e] = r[e]

    pl.semaphore_wait(barrier, total + jnp.where(me > 0, 1, 0) + jnp.where(me < n - 1, 1, 0))
    halo_start(0)
    reduce_start(0, 0, b_part)

    def spread_rows(raw):
        left[...] = raw[:, :, 0:half].astype(F32).reshape(left.shape)
        right[:, 0 : width - half] = (
            raw[:, :, half:width].astype(F32).reshape(width * elements, width - half)
        )

    def block_of(e):
        rows = pl.ds(e, width, stride=elements)
        return jnp.concatenate([left[rows, :], right[rows, :]], axis=1)

    def take_apart(k, carry):
        pltpu.make_async_copy(jac_hbm.at[k], jraw.at[k], jsem.at[k]).wait()
        spread_rows(jraw[k])
        for e in range(elements):
            block = block_of(e)[:, 0:width].astype(BF16)
            jac[k, e] = block
            jac_t[k, e] = block.T
        return carry

    lax.fori_loop(0, faces1, take_apart, 0)
    wcopy.wait()
    spread_rows(wraw[...])
    for e in range(elements):
        wgt_t[e] = block_of(e)[:, 0:width].astype(BF16).T

    def forward(t):
        y = []
        for e in range(elements):
            acc = dot_rows(xs[t, e].astype(BF16), jac_t[0, e])
            for k in range(1, faces1):
                acc = acc + dot_rows(xs[t, nbr[e][k - 1]].astype(BF16), jac_t[k, e])
            y.append(acc.astype(BF16))
        return [dot_rows(y[e], wgt_t[e]).astype(BF16) for e in range(elements)]

    def backward(z):
        acc = [jnp.zeros(rows_shape, F32) for _ in range(slots)]
        for e in range(elements):
            acc[e] = acc[e] + dot_rows(z[e], jac[0, e])
            for k in range(1, faces1):
                term = dot_rows(z[e], jac[k, e])
                for m in range(slots):
                    acc[m] = acc[m] + jnp.where(nbr[e][k - 1] == m, term, 0.0)
        return acc

    def send_partials(t, acc):
        for m in range(slots):
            up[t, m] = acc[m]
        for side in range(2):
            for s in range(cap):
                if t < 3:
                    hsend[t, side, s] = up[t, lists[side][s]]
                hsend[t, side, cap + s] = acc[elements + side * cap + s]
        halo_start(t)

    def merged(t, m):
        value = up[t, m]
        for side in range(2):
            for s in range(cap):
                value = value + jnp.where(lists[side][s] == m, hrecv[t, side, cap + s], 0.0)
        return value

    def receive_partials(t, factor=1.0):
        for m in range(elements):
            xs[t, m] = merged(t, m) * factor
        for side in range(2):
            for s in range(cap):
                m = elements + side * cap + s
                xs[t, m] = (up[t, m] + hrecv[t, side, s]) * factor

    halo_wait(0)
    for side in range(2):
        for s in range(cap):
            xs[0, elements + side * cap + s] = hrecv[0, side, s]
    send_partials(1, backward(forward(0)))
    for stage in range(stages - 1):
        reduce_start(0, stage + 1, reduce_end(0, stage)[0])
    halo_wait(1)
    receive_partials(1)
    span = range(elements)
    flow = jnp.zeros(isend.shape, F32)
    ilane = lax.broadcasted_iota(jnp.int32, isend.shape, 1)
    for e in span:
        row = flow_ref[pl.ds(e, 1), :]
        flow = jnp.where(ilane == e, jnp.sum(rhs_ref[e] * row, axis=1, keepdims=True), flow)
        flow = jnp.where(
            ilane == elements + e, jnp.sum(xs[1, e] * row, axis=1, keepdims=True), flow
        )
    isend[...] = flow
    icopies = [
        pltpu.make_async_remote_copy(
            src_ref=isend,
            dst_ref=irecv.at[o - 1],
            send_sem=is_sem.at[o - 1],
            recv_sem=ir_sem.at[o - 1],
            device_id=(me, lax.rem(core + o, cores)),
            device_id_type=MESH,
        )
        for o in range(1, cores)
    ]
    for copy in icopies:
        copy.start()
    send_partials(2, backward(forward(1)))
    b_sums = [v[:, 0:1] for v in reduce_end(0, stages - 1)]
    betas = [jnp.sqrt(v + EPSILON) for v in b_sums]
    scales = [1.0 / v for v in betas]
    scale = scales[0]
    v1 = [rhs_ref[e] * scale for e in span]
    raw = [xs[1, e] * scale for e in span]
    halo_wait(2)
    receive_partials(2, scale)
    u2 = [xs[2, e] for e in span]
    grams = packed(
        [
            inner(zip(v1, raw)),
            inner(zip(raw, raw)),
            inner(zip(v1, u2)),
            inner(zip(raw, u2)),
            inner(zip(u2, u2)),
        ]
    )
    reduce_start(1, 0, grams)
    send_partials(3, backward(forward(2)))
    for stage in range(stages - 1):
        reduce_start(1, stage + 1, reduce_end(1, stage)[0])
    all_sums = reduce_end(1, stages - 1)
    for copy in icopies:
        copy.wait()
    ind = None
    for o in range(cores):
        sums = [all_sums[o][:, i : i + 1] for i in range(5)]
        a0, a1 = coefficients(betas[o], b_sums[o] * scales[o] * scales[o], *sums)
        flow = isend[...] if o == 0 else irecv[o - 1]
        dots = a0 * scales[o] * flow[:, 0:elements] + a1 * scales[o] * flow[:, elements : 2 * elements]
        term = jnp.sum(jnp.abs(dots), axis=0, keepdims=True)
        ind = term if ind is None else ind + term
        if o == 0:
            own0, own1 = a0, a1
    ind_ref[...] = ind
    k0 = own0 * scale
    k1 = own1 * scale
    for e in span:
        adj_ref[e] = k0 * rhs_ref[e] + k1 * xs[1, e]
    k1 = 1.0 + k0
    k2 = own1 - own0
    halo_wait(3)
    for e in span:
        res_ref[e] = rhs_ref[e] - (k1 * xs[1, e] + k2 * xs[2, e] - own1 * merged(3, e))
    for t in range(4):
        halo_finish(t)


def per_device(n, jacobian, block_weight, rhs_grad, flow_residual, face_nbr, send_list):
    elements, faces1, width = jacobian.shape[:3]
    rows = rhs_grad.shape[1:]
    cap = send_list.shape[2]
    slots = elements + 2 * cap
    radices = radices_of(n)
    stages, widest = len(radices), max(radices)
    cores = lax.axis_size("rhs")
    vmem = pl.BlockSpec(memory_space=pltpu.VMEM)
    smem = pl.BlockSpec(memory_space=pltpu.SMEM)
    anywhere = pl.BlockSpec(memory_space=pl.ANY)
    adjoint, residual, indicator = pl.pallas_call(
        functools.partial(kernel, n, radices),
        out_shape=(
            jax.ShapeDtypeStruct(rhs_grad.shape, F32),
            jax.ShapeDtypeStruct(rhs_grad.shape, F32),
            jax.ShapeDtypeStruct((1, elements), F32),
        ),
        in_specs=[anywhere, anywhere, vmem, vmem, smem, smem],
        out_specs=(vmem, vmem, vmem),
        scratch_shapes=[
            pltpu.VMEM((faces1, width, elements, width), BF16),
            pltpu.VMEM((width, elements, width), BF16),
            pltpu.VMEM((faces1, elements, width, width), BF16),
            pltpu.VMEM((faces1, elements, width, width), BF16),
            pltpu.VMEM((elements, width, width), BF16),
            pltpu.VMEM((width * elements, 128), F32),
            pltpu.VMEM((width * elements, 128), F32),
            pltpu.VMEM((3, slots) + rows, F32),
            pltpu.VMEM((4, slots) + rows, F32),
            pltpu.VMEM((4, 2, 2 * cap) + rows, F32),
            pltpu.VMEM((4, 2, 2 * cap) + rows, F32),
            pltpu.VMEM((2, stages, rows[0], 128), F32),
            pltpu.VMEM((2, stages, cores, widest, rows[0], 128), F32),
            pltpu.VMEM((rows[0], 128), F32),
            pltpu.VMEM((max(cores - 1, 1), rows[0], 128), F32),
            pltpu.SemaphoreType.DMA((faces1,)),
            pltpu.SemaphoreType.DMA,
            pltpu.SemaphoreType.DMA((4, 2)),
            pltpu.SemaphoreType.DMA((4, 2)),
            pltpu.SemaphoreType.DMA((2, stages, cores, widest)),
            pltpu.SemaphoreType.DMA((2, stages, cores, widest)),
            pltpu.SemaphoreType.DMA((max(cores - 1, 1),)),
            pltpu.SemaphoreType.DMA((max(cores - 1, 1),)),
        ],
        compiler_params=pltpu.CompilerParams(
            collective_id=0, has_side_effects=True, vmem_limit_bytes=56 * 2**20
        ),
    )(
        jnp.transpose(jacobian, (1, 2, 0, 3)), jnp.transpose(block_weight, (1, 0, 2)), rhs_grad, flow_residual, face_nbr, send_list)
    return adjoint, residual, indicator.reshape(elements)


def solution(mesh):
    in_specs = (
        P("dom", None, None, None),
        P("dom", None, None),
        P("dom", "rhs", None),
        P("dom", None),
        P("dom", None),
        P("dom", None, None),
    )
    out_specs = (P("dom", "rhs", None), P("dom", "rhs", None), P("dom"))
    return jax.shard_map(
        functools.partial(per_device, mesh.shape["dom"]),
        mesh=mesh,
        in_specs=in_specs,
        out_specs=out_specs,
        check_vma=False,
    )
```

```python
import functools

import jax
import jax.numpy as jnp
from jax import lax
from jax.experimental import pallas as pl
from jax.experimental.pallas import tpu as pltpu
from jax.sharding import PartitionSpec as P

EPSILON = 1e-06
EARLY = 2
MESH = pl.DeviceIdType.MESH
F32 = jnp.float32
BF16 = jnp.bfloat16


def radices_of(n):
    out = []
    while n > 1:
        for r in (4, 2, 3, 5, 7):
            if n % r == 0:
                out.append(r)
                n //= r
                break
        else:
            out.append(n)
            n = 1
    return out


def dot_rows(rows, block):
    return lax.dot_general(rows, block, (((1,), (0,)), ((), ())), preferred_element_type=F32)


def coefficients(beta, b, c, d, e, f, g):
    h11 = c
    w_sq = d - 2.0 * h11 * c + h11 * h11 * b
    h21 = jnp.sqrt(jnp.maximum(w_sq, 0.0) + EPSILON)
    s = 1.0 / h21
    h12 = s * (e - h11 * c)
    v2v1 = s * (c - h11 * b)
    v2v2 = s * s * w_sq
    v2raw2 = s * s * (f - h11 * d - h11 * e + h11 * h11 * c)
    raw2sq = s * s * (g - 2.0 * h11 * f + h11 * h11 * d)
    h22 = v2raw2 - h12 * v2v1
    last = (
        raw2sq
        + h12 * h12 * b
        + h22 * h22 * v2v2
        - 2.0 * h12 * h12
        - 2.0 * h22 * v2raw2
        + 2.0 * h12 * h22 * v2v1
    )
    h32 = jnp.sqrt(jnp.maximum(last, 0.0) + EPSILON)
    radius = jnp.sqrt(h11 * h11 + h21 * h21)
    cos1, sin1 = h11 / radius, h21 / radius
    t1, t2 = cos1 * beta, -sin1 * beta
    upper = cos1 * h12 + sin1 * h22
    low = -sin1 * h12 + cos1 * h22
    radius2 = jnp.sqrt(low * low + h32 * h32)
    t2 = (low / radius2) * t2
    c2 = t2 / radius2
    c1 = (t1 - upper * c2) / radius
    return c1 - c2 * s * h11, c2 * s


def kernel(
    n, radices,
    jac_hbm, wgt_hbm, rhs_ref, flow_ref, nbr_ref, list_ref,
    adj_ref, res_ref, ind_ref,
    jraw, wraw, jac, jac_t, wgt_t, left, right, xs, up, hsend, hrecv, asend, arecv, isend, irecv,
    jsem, wsem, hs_sem, hr_sem, as_sem, ar_sem, is_sem, ir_sem,
):
    faces1, elements = jac.shape[0], jac.shape[1]
    width = jac.shape[2]
    half = left.shape[1]
    cap = list_ref.shape[2]
    slots = elements + 2 * cap
    me = lax.axis_index("dom")
    core = lax.axis_index("rhs")
    cores = lax.axis_size("rhs")

    for k in range(faces1):
        pltpu.make_async_copy(jac_hbm.at[k], jraw.at[k], jsem.at[k]).start()
    wcopy = pltpu.make_async_copy(wgt_hbm, wraw, wsem)
    wcopy.start()

    strides = []
    stride = 1
    for radix in radices:
        strides.append(stride)
        stride *= radix

    def partner(stage, offset):
        radix, step = radices[stage], strides[stage]
        digit = lax.rem(lax.div(me, step), radix)
        return me + (lax.rem(digit + offset, radix) - digit) * step

    stages = len(radices)

    def peers(stage):
        spread = cores if stage == stages - 1 else 1
        out = []
        for offset in range(radices[stage]):
            for other in range(spread):
                if offset or other:
                    target = partner(stage, offset) if offset else me
                    out.append((offset, other, (target, lax.rem(core + other, cores))))
        return out

    barrier = pltpu.get_barrier_semaphore()
    total = 0
    for stage in range(stages):
        for _, _, target in peers(stage):
            pl.semaphore_signal(barrier, inc=1, device_id=target, device_id_type=MESH)
            total += 1

    @pl.when(me > 0)
    def _():
        pl.semaphore_signal(barrier, inc=1, device_id=(me - 1, core), device_id_type=MESH)

    @pl.when(me < n - 1)
    def _():
        pl.semaphore_signal(barrier, inc=1, device_id=(me + 1, core), device_id_type=MESH)

    rows_shape = rhs_ref.shape[1:]

    height = rows_shape[0]
    blank = jnp.zeros((hrecv.shape[0],) + hrecv.shape[2:], BF16)

    @pl.when(me == 0)
    def _():
        hrecv[:, 0] = blank

    @pl.when(me == n - 1)
    def _():
        hrecv[:, 1] = blank

    lists = [[list_ref[0, side, s] for s in range(cap)] for side in range(2)]
    nbr = [[nbr_ref[e, k] for k in range(faces1 - 1)] for e in range(elements)]

    part = cap * height
    ranges = ((0, part), (0, 2 * part), (0, 2 * part), (part, part))

    def halo(t, side):
        first, count = ranges[t]
        target = me - 1 if side == 0 else me + 1
        return pltpu.make_async_remote_copy(
            src_ref=hsend.at[t, side, pl.ds(first, count)],
            dst_ref=hrecv.at[t, 1 - side, pl.ds(first, count)],
            send_sem=hs_sem.at[t, side],
            recv_sem=hr_sem.at[t, 1 - side],
            device_id=(target, core),
            device_id_type=MESH,
        )

    def halo_start(t):
        @pl.when(me > 0)
        def _():
            halo(t, 0).start()

        @pl.when(me < n - 1)
        def _():
            halo(t, 1).start()

    def halo_wait(t):
        @pl.when(me > 0)
        def _():
            halo(t, 1).wait_recv()

        @pl.when(me < n - 1)
        def _():
            halo(t, 0).wait_recv()

    def halo_finish(t):
        @pl.when(me > 0)
        def _():
            halo(t, 0).wait_send()

        @pl.when(me < n - 1)
        def _():
            halo(t, 1).wait_send()

    def reduce_copies(q, stage):
        return [
            pltpu.make_async_remote_copy(
                src_ref=asend.at[q, stage],
                dst_ref=arecv.at[q, stage, other, offset],
                send_sem=as_sem.at[q, stage, other, offset],
                recv_sem=ar_sem.at[q, stage, other, offset],
                device_id=target,
                device_id_type=MESH,
            )
            for offset, other, target in peers(stage)
        ]

    def reduce_start(q, stage, value):
        asend[q, stage] = value
        for copy in reduce_copies(q, stage):
            copy.start()

    def reduce_end(q, stage):
        for copy in reduce_copies(q, stage):
            copy.wait()
        sums = []
        for other in range(cores if stage == stages - 1 else 1):
            value = arecv[q, stage, other, 0] if other else asend[q, stage]
            for offset in range(1, radices[stage]):
                value = value + arecv[q, stage, other, offset]
            sums.append(value)
        return sums

    lane = lax.broadcasted_iota(jnp.int32, asend.shape[2:], 1)

    def packed(columns):
        out = jnp.zeros(asend.shape[2:], F32)
        for i, column in enumerate(columns):
            out = jnp.where(lane == i, column, out)
        return out

    def inner(pairs):
        acc = None
        for a, b in pairs:
            acc = a * b if acc is None else acc + a * b
        return jnp.sum(acc, axis=1, keepdims=True)

    r = [rhs_ref[e] for e in range(elements)]
    b_part = packed([inner([(v, v) for v in r])])
    for side in range(2):
        chosen = [rhs_ref[lists[side][s]] for s in range(cap)]
        hsend[0, side, 0:part] = jnp.concatenate(chosen, axis=0).astype(BF16)
    for e in range(elements):
        xs[0, e] = r[e]

    def spread_rows(raw):
        left[...] = raw[:, :, 0:half].astype(F32).reshape(left.shape)
        right[:, 0 : width - half] = (
            raw[:, :, half:width].astype(F32).reshape(width * elements, width - half)
        )

    def block_of(e):
        rows = pl.ds(e, width, stride=elements)
        return jnp.concatenate([left[rows, :], right[rows, :]], axis=1)

    def take_apart(k, carry):
        pltpu.make_async_copy(jac_hbm.at[k], jraw.at[k], jsem.at[k]).wait()
        spread_rows(jraw[k])
        for e in range(elements):
            block = block_of(e)[:, 0:width].astype(BF16)
            jac[k, e] = block
            jac_t[k, e] = block.T
        return carry

    lax.fori_loop(0, EARLY, take_apart, 0)
    pl.semaphore_wait(barrier, total + jnp.where(me > 0, 1, 0) + jnp.where(me < n - 1, 1, 0))
    halo_start(0)
    reduce_start(0, 0, b_part)

    lax.fori_loop(EARLY, faces1, take_apart, 0)
    wcopy.wait()
    spread_rows(wraw[...])
    for e in range(elements):
        wgt_t[e] = block_of(e)[:, 0:width].astype(BF16).T

    def forward(t):
        y = []
        for e in range(elements):
            acc = dot_rows(xs[t, e].astype(BF16), jac_t[0, e])
            for k in range(1, faces1):
                acc = acc + dot_rows(xs[t, nbr[e][k - 1]].astype(BF16), jac_t[k, e])
            y.append(acc.astype(BF16))
        return [dot_rows(y[e], wgt_t[e]).astype(BF16) for e in range(elements)]

    def backward(z):
        acc = [jnp.zeros(rows_shape, F32) for _ in range(slots)]
        for e in range(elements):
            acc[e] = acc[e] + dot_rows(z[e], jac[0, e])
            for k in range(1, faces1):
                term = dot_rows(z[e], jac[k, e])
                for m in range(slots):
                    acc[m] = acc[m] + jnp.where(nbr[e][k - 1] == m, term, 0.0)
        return acc

    def send_partials(t, acc):
        for m in range(slots):
            up[t, m] = acc[m]
        for side in range(2):
            first = elements + side * cap
            terms = jnp.concatenate(acc[first : first + cap], axis=0)
            hsend[t, side, part : 2 * part] = terms.astype(BF16)
            if t < 3:
                owned = jnp.concatenate([up[t, lists[side][s]] for s in range(cap)], axis=0)
                hsend[t, side, 0:part] = owned.astype(BF16)
        halo_start(t)

    def arrived(t, side, first):
        rows = hrecv[t, side, first : first + part].astype(F32)
        return [rows[s * height : (s + 1) * height] for s in range(cap)]

    def merged(t):
        values = [up[t, m] for m in range(elements)]
        for side in range(2):
            for s, term in enumerate(arrived(t, side, part)):
                for m in range(elements):
                    values[m] = values[m] + jnp.where(lists[side][s] == m, term, 0.0)
        return values

    def receive_partials(t, factor=1.0):
        for m, value in enumerate(merged(t)):
            xs[t, m] = value * factor
        for side in range(2):
            for s, term in enumerate(arrived(t, side, 0)):
                m = elements + side * cap + s
                xs[t, m] = (up[t, m] + term) * factor

    halo_wait(0)
    for side in range(2):
        for s, term in enumerate(arrived(0, side, 0)):
            xs[0, elements + side * cap + s] = term
    send_partials(1, backward(forward(0)))
    for stage in range(stages - 1):
        reduce_start(0, stage + 1, reduce_end(0, stage)[0])
    halo_wait(1)
    receive_partials(1)
    span = range(elements)
    flow = jnp.zeros(isend.shape, F32)
    ilane = lax.broadcasted_iota(jnp.int32, isend.shape, 1)
    for e in span:
        row = flow_ref[pl.ds(e, 1), :]
        flow = jnp.where(ilane == e, jnp.sum(rhs_ref[e] * row, axis=1, keepdims=True), flow)
        flow = jnp.where(
            ilane == elements + e, jnp.sum(xs[1, e] * row, axis=1, keepdims=True), flow
        )
    isend[...] = flow
    icopies = [
        pltpu.make_async_remote_copy(
            src_ref=isend,
            dst_ref=irecv.at[o - 1],
            send_sem=is_sem.at[o - 1],
            recv_sem=ir_sem.at[o - 1],
            device_id=(me, lax.rem(core + o, cores)),
            device_id_type=MESH,
        )
        for o in range(1, cores)
    ]
    for copy in icopies:
        copy.start()
    send_partials(2, backward(forward(1)))
    b_sums = [v[:, 0:1] for v in reduce_end(0, stages - 1)]
    betas = [jnp.sqrt(v + EPSILON) for v in b_sums]
    scales = [1.0 / v for v in betas]
    scale = scales[0]
    v1 = [rhs_ref[e] * scale for e in span]
    raw = [xs[1, e] * scale for e in span]
    halo_wait(2)
    receive_partials(2, scale)
    u2 = [xs[2, e] for e in span]
    grams = packed(
        [
            inner(zip(v1, raw)),
            inner(zip(raw, raw)),
            inner(zip(v1, u2)),
            inner(zip(raw, u2)),
            inner(zip(u2, u2)),
        ]
    )
    reduce_start(1, 0, grams)
    send_partials(3, backward(forward(2)))
    for stage in range(stages - 1):
        reduce_start(1, stage + 1, reduce_end(1, stage)[0])
    all_sums = reduce_end(1, stages - 1)
    for copy in icopies:
        copy.wait()
    ind = None
    for o in range(cores):
        sums = [all_sums[o][:, i : i + 1] for i in range(5)]
        a0, a1 = coefficients(betas[o], b_sums[o] * scales[o] * scales[o], *sums)
        flow = isend[...] if o == 0 else irecv[o - 1]
        dots = a0 * scales[o] * flow[:, 0:elements] + a1 * scales[o] * flow[:, elements : 2 * elements]
        term = jnp.sum(jnp.abs(dots), axis=0, keepdims=True)
        ind = term if ind is None else ind + term
        if o == 0:
            own0, own1 = a0, a1
    ind_ref[...] = ind
    k0 = own0 * scale
    k1 = own1 * scale
    for e in span:
        adj_ref[e] = k0 * rhs_ref[e] + k1 * xs[1, e]
    k1 = 1.0 + k0
    k2 = own1 - own0
    halo_wait(3)
    for e, value in enumerate(merged(3)):
        res_ref[e] = rhs_ref[e] - (k1 * xs[1, e] + k2 * xs[2, e] - own1 * value)
    for t in range(4):
        halo_finish(t)


def write_out(a_in, b_in, c_in, a_out, b_out, c_out, sems):
    pairs = ((a_in, a_out), (b_in, b_out), (c_in, c_out))
    copies = [pltpu.make_async_copy(src, dst, sems.at[i]) for i, (src, dst) in enumerate(pairs)]
    for copy in copies:
        copy.start()
    for copy in copies:
        copy.wait()


def per_device(n, jacobian, block_weight, rhs_grad, flow_residual, face_nbr, send_list):
    elements, faces1, width = jacobian.shape[:3]
    rows = rhs_grad.shape[1:]
    cap = send_list.shape[2]
    slots = elements + 2 * cap
    radices = radices_of(n)
    stages, widest = len(radices), max(radices)
    cores = lax.axis_size("rhs")
    vmem = pl.BlockSpec(memory_space=pltpu.VMEM)
    smem = pl.BlockSpec(memory_space=pltpu.SMEM)
    anywhere = pl.BlockSpec(memory_space=pltpu.HBM)
    adjoint, residual, indicator = pl.pallas_call(
        functools.partial(kernel, n, radices),
        out_shape=(
            jax.ShapeDtypeStruct(rhs_grad.shape, F32),
            jax.ShapeDtypeStruct(rhs_grad.shape, F32),
            jax.ShapeDtypeStruct((1, elements), F32),
        ),
        in_specs=[anywhere, anywhere, vmem, vmem, smem, smem],
        out_specs=(vmem, vmem, vmem),
        scratch_shapes=[
            pltpu.VMEM((faces1, width, elements, width), BF16),
            pltpu.VMEM((width, elements, width), BF16),
            pltpu.VMEM((faces1, elements, width, width), BF16),
            pltpu.VMEM((faces1, elements, width, width), BF16),
            pltpu.VMEM((elements, width, width), BF16),
            pltpu.VMEM((width * elements, 128), F32),
            pltpu.VMEM((width * elements, 128), F32),
            pltpu.VMEM((3, slots) + rows, F32),
            pltpu.VMEM((4, slots) + rows, F32),
            pltpu.VMEM((4, 2, 2 * cap * rows[0], width), BF16),
            pltpu.VMEM((4, 2, 2 * cap * rows[0], width), BF16),
            pltpu.VMEM((2, stages, rows[0], 128), F32),
            pltpu.VMEM((2, stages, cores, widest, rows[0], 128), F32),
            pltpu.VMEM((rows[0], 128), F32),
            pltpu.VMEM((max(cores - 1, 1), rows[0], 128), F32),
            pltpu.SemaphoreType.DMA((faces1,)),
            pltpu.SemaphoreType.DMA,
            pltpu.SemaphoreType.DMA((4, 2)),
            pltpu.SemaphoreType.DMA((4, 2)),
            pltpu.SemaphoreType.DMA((2, stages, cores, widest)),
            pltpu.SemaphoreType.DMA((2, stages, cores, widest)),
            pltpu.SemaphoreType.DMA((max(cores - 1, 1),)),
            pltpu.SemaphoreType.DMA((max(cores - 1, 1),)),
        ],
        compiler_params=pltpu.CompilerParams(
            collective_id=0, has_side_effects=True, vmem_limit_bytes=50 * 2**20
        ),
    )(
        jnp.transpose(jacobian, (1, 2, 0, 3)), jnp.transpose(block_weight, (1, 0, 2)), rhs_grad, flow_residual, face_nbr, send_list)
    results = (adjoint, residual, indicator)
    adjoint, residual, indicator = pl.pallas_call(
        write_out,
        out_shape=tuple(jax.ShapeDtypeStruct(v.shape, F32) for v in results),
        in_specs=[pl.BlockSpec(memory_space=pl.ANY)] * 3,
        out_specs=(anywhere,) * 3,
        scratch_shapes=[pltpu.SemaphoreType.DMA((3,))],
        compiler_params=pltpu.CompilerParams(vmem_limit_bytes=2 * 2**20),
    )(*results)
    return adjoint, residual, indicator.reshape(elements)


def solution(mesh):
    in_specs = (
        P("dom", None, None, None),
        P("dom", None, None),
        P("dom", "rhs", None),
        P("dom", None),
        P("dom", None),
        P("dom", None, None),
    )
    out_specs = (P("dom", "rhs", None), P("dom", "rhs", None), P("dom"))
    return jax.shard_map(
        functools.partial(per_device, mesh.shape["dom"]),
        mesh=mesh,
        in_specs=in_specs,
        out_specs=out_specs,
        check_vma=False,
    )
```
